128 devices in a mesh: freq: 16 (over x_hi, y, core), stn: 8 (over x_lo, z).
Axes of the slice: x: 4 (x_hi: 2, x_lo: 2; x = x_hi * 2 + x_lo), y: 4, z: 4, core: 2. Of those that a mesh axis runs over, the one named last changes fastest.
Arguments:
- voltages: bfloat16 [1024, 32, 4096], P('stn', 'freq'), may hold values from -6 to 6
- filter_taps: float32 [16, 4096], replicated, may hold values from -1.5 to 1.5
- station_flags: int32 [512, 32], replicated, may hold values from 0 to 1, as said below
Outputs:
- visibilities: float32 [256, 1024, 1024], P('freq', 'stn')
The draws below stay inside these ranges and needn't reach their ends.
Inputs may be any that keep to these rules, and one draw needn't show every extreme that they name: `station_flags`: 1 keeps a station's data in that spectrum, 0 flags it.
All inputs are finite; a program needn't handle non-finite values.
Results may differ from the reference program's by a relative error of at most 0.0039.
Values may be sent and summed in bfloat16 or wider, within the bound.
No kernel may reach another device: no remote copies, remote signals or barrier semaphores. Data moves between devices by JAX's collectives and lax.ppermute only.
A program may use at most 192 MiB of HBM per device.

```python
import math
import jax
import jax.numpy as jnp
from jax import lax

C = 4096
TAPS = 16
AVG = 16
STATIONS = 512
SIGNALS = 1024
SPECTRA = 32
GROUPS = 256
N_STN = 8


def draw_station_flags(key, part):
    key = jax.random.fold_in(key, 5)
    first_key, second_key = jax.random.split(key)
    levels = jax.random.randint(first_key, (STATIONS, 1), 0, 9)
    rolls = jax.random.randint(second_key, (STATIONS, SPECTRA), 0, 8)
    return (rolls < levels).astype(jnp.int32)


def block_scale(key, shape, cuts, low, high):
    level, own = 1.0, jax.random.fold_in(key, 6)
    for position, shards_of in cuts:
        heights = jnp.exp(jax.random.uniform(jax.random.fold_in(own, position), (shards_of,), jnp.float32, low / len(cuts), high / len(cuts)))
        level = level * jnp.repeat(heights, shape[position] // shards_of).reshape([-1 if axis == position else 1 for axis in range(len(shape))])
    return level


def noise(key, shape, scale, most, pieces=(), kind=jnp.bfloat16):
    array = jax.random.normal(key, shape, jnp.float32) * scale
    if len(pieces) > 0:
        array = block_scale(key, shape, pieces, -0.22, 0.18) * array
    return jnp.clip(array, min=-most, max=most).astype(kind)


def setup_inputs(seed: int = 0) -> dict:
    key_list = jax.random.split(jax.random.key(seed), 4)
    voltages = noise(key_list[0], (SIGNALS, SPECTRA, C), 1.0, 6.0, ((0, 8), (1, 16)))
    filter_taps = noise(key_list[1], (TAPS, C), TAPS ** -0.5, 1.5, (), jnp.float32)
    station_flags = draw_station_flags(jax.random.fold_in(key_list[3], 71), 0)
    return dict(voltages=voltages, filter_taps=filter_taps, station_flags=station_flags)


def channelize(signal_block, filter_taps):
    padded = jnp.pad(signal_block.astype(jnp.float32), ((0, 0), (TAPS - 1, 0), (0, 0)))
    window = jnp.zeros(signal_block.shape, jnp.float32)
    for tap_index in range(TAPS):
        offset = TAPS - 1 - tap_index
        window = window + filter_taps[tap_index][None, None, :] * padded[:, offset:offset + SPECTRA, :]
    positions = jnp.arange(C).astype(jnp.float32)
    pre_angle = math.pi * positions / (2 * C)
    twisted = window * jnp.cos(pre_angle) - 1j * (window * jnp.sin(pre_angle))
    spectrum = jnp.fft.fft(twisted, axis=-1)
    post_angle = math.pi * (2 * positions + 1) / (4 * C)
    result = math.sqrt(2.0 / C) * (jnp.real(spectrum) * jnp.cos(post_angle) + jnp.imag(spectrum) * jnp.sin(post_angle))
    return result.astype(jnp.bfloat16)

def reference(voltages, filter_taps, station_flags):
    per_block = SIGNALS // N_STN
    grouped = voltages.reshape(N_STN, per_block, SPECTRA, C)
    channelized = lax.map(lambda part_block: channelize(part_block, filter_taps), grouped)
    channelized = channelized.reshape(SIGNALS, SPECTRA, C)
    keep = jnp.repeat(station_flags, 2, axis=0).astype(jnp.float32)
    kept = channelized * keep[:, :, None].astype(jnp.bfloat16)
    counts = jnp.dot(keep, keep.T, precision=lax.Precision.HIGHEST)
    arranged = kept.reshape(SIGNALS, SPECTRA, GROUPS, AVG).transpose(2, 0, 1, 3).reshape(GROUPS, SIGNALS, SPECTRA * AVG)
    sums = lax.map(lambda rows_group: jnp.dot(rows_group, rows_group.T, preferred_element_type=jnp.float32), arranged)
    return sums / (AVG * jnp.maximum(counts, 1.0))[None]
```

```python
import math

import jax
import jax.numpy as jnp
import numpy as np
from jax import lax
from jax.experimental import pallas as pl
from jax.experimental.pallas import tpu as pltpu
from jax.sharding import PartitionSpec as P

AVG = 16
LANES = 128
INNER = 256
F32 = jnp.float32
BF16 = jnp.bfloat16


def transform_tables(channels, n_freq, n_stn):
    j0 = np.arange(INNER, dtype=np.float64)
    k1 = np.arange(AVG, dtype=np.float64)
    phase = 2 * np.pi * k1[:, None] * j0[None, :] / channels + np.pi * j0[None, :] / (2 * channels)
    phase = phase + np.pi * (2 * k1[:, None] + 1) / (4 * channels)
    twiddle = np.stack([np.cos(phase), -np.sin(phase)]).astype(np.float32)
    groups = channels // AVG
    per_device = groups // (n_freq * n_stn)
    k2 = np.arange(groups).reshape(n_freq, n_stn, per_device).transpose(1, 0, 2).reshape(-1)
    phase = 2 * np.pi * (k2[:, None] * np.arange(INNER)[None, :] % INNER) / INNER
    phase = phase + 2 * np.pi * AVG * k2[:, None] / (4 * channels)
    scale = math.sqrt(2.0 / channels)
    exact = np.concatenate([np.cos(phase), np.sin(phase)], axis=1) * scale
    exact = jnp.asarray(exact.astype(np.float32))
    high = exact.astype(BF16)
    low = (exact - high.astype(F32)).astype(BF16)
    return jnp.asarray(twiddle), jnp.concatenate([high, high, low], axis=1)


def times(value, angle):
    c, s = math.cos(angle), math.sin(angle)
    re, im = value
    return re * c + im * s, im * c - re * s


def four_point(u0, u1, u2, u3):
    def add(a, b):
        return a[0] + b[0], a[1] + b[1]

    def sub(a, b):
        return a[0] - b[0], a[1] - b[1]

    s0, s1, t0, t1 = add(u0, u2), sub(u0, u2), add(u1, u3), sub(u1, u3)
    return add(s0, t0), (s1[0] + t1[1], s1[1] - t1[0]), sub(s0, t0), (s1[0] - t1[1], s1[1] + t1[0])


def sixteen_point(x):
    mid = []
    for b in range(4):
        u = [(x[b], jnp.zeros_like(x[b]))]
        for a in range(1, 4):
            angle = math.pi * a / 8
            u.append((x[4 * a + b] * math.cos(angle), x[4 * a + b] * -math.sin(angle)))
        row = four_point(*u)
        mid.append([times(row[p], 2 * math.pi * b * p / 16 + math.pi * b / 32) if b else row[p] for p in range(4)])
    y = [None] * 16
    for p in range(4):
        out = four_point(*[mid[b][p] for b in range(4)])
        for q in range(4):
            y[p + 4 * q] = out[q]
    return y


def channelize_kernel(x_ref, taps_ref, twiddle_ref, second_ref, keep_ref, out_ref, window, stage, turned):
    frames, signals, channels = x_ref.shape
    taps = taps_ref.shape[0]
    groups = second_ref.shape[0]

    def fir(block, carry):
        lanes = pl.ds(pl.multiple_of(block * LANES, LANES), LANES)
        tap = [jnp.broadcast_to(taps_ref[pl.ds(t, 1), lanes], (signals, LANES)) for t in range(taps)]
        x = [x_ref[m, :, lanes].astype(F32) for m in range(frames)]
        for m in range(frames):
            total = tap[0] * x[m]
            for t in range(1, min(taps, m + 1)):
                total = total + tap[t] * x[m - t]
            window[m, :, lanes] = total
        return carry

    lax.fori_loop(0, channels // LANES, fir, 0)

    def first(m, carry):
        for half in range(INNER // LANES):
            at = pl.ds(half * LANES, LANES)
            x = [window[m, :, pl.ds(j1 * INNER + half * LANES, LANES)] for j1 in range(AVG)]
            for k1, y in enumerate(sixteen_point(x)):
                tre = twiddle_ref[0, pl.ds(k1, 1), at]
                tim = twiddle_ref[1, pl.ds(k1, 1), at]
                rows = pl.ds(pl.multiple_of(k1 * frames * signals + m * signals, signals), signals)
                stage[half, rows, :] = y[0] * tre - y[1] * tim
                stage[INNER // LANES + half, rows, :] = y[0] * tim + y[1] * tre
        return carry

    lax.fori_loop(0, frames, first, 0)

    columns = AVG * frames
    for i in range(signals):
        y = jnp.concatenate([stage[part, pl.ds(i, columns, stride=signals), :] for part in range(4)], axis=1)
        high = y.astype(BF16)
        low = (y - high.astype(F32)).astype(BF16)
        z = lax.dot_general(
            second_ref[...],
            jnp.concatenate([high, low, high], axis=1),
            (((1,), (1,)), ((), ())),
            preferred_element_type=F32,
        )
        for c in range(columns // LANES):
            turned[c, pl.ds(i, groups, stride=signals), :] = z[:, c * LANES : (c + 1) * LANES]

    keep = keep_ref[...]

    def last(step, carry):
        rows = pl.ds(pl.multiple_of(step * 32 * signals, 32 * signals), 32 * signals)
        for c in range(columns // LANES):
            value = turned[c, rows, :].reshape(16, 2, signals, LANES) * keep[None, None]
            for pair in range(2):
                part = value[:, pair].reshape(16 * signals, LANES).astype(BF16)
                to = pl.ds(pl.multiple_of(step * 16 * signals, 16 * signals), 16 * signals)
                out_ref[to, pair * columns + c * LANES : pair * columns + (c + 1) * LANES] = part
        return carry

    lax.fori_loop(0, groups // 32, last, 0)


def channelize(x, taps, twiddle, second, keep):
    frames, signals, channels = x.shape
    groups = channels // AVG
    columns = AVG * frames
    whole = pl.BlockSpec(memory_space=pltpu.VMEM)
    return pl.pallas_call(
        channelize_kernel,
        out_shape=jax.ShapeDtypeStruct((groups // 2 * signals, 2 * columns), BF16),
        in_specs=[whole] * 5,
        out_specs=whole,
        scratch_shapes=[
            pltpu.VMEM((frames, signals, channels), F32),
            pltpu.VMEM((4, AVG * frames * signals, LANES), F32),
            pltpu.VMEM((columns // LANES, groups * signals, LANES), F32),
        ],
        compiler_params=pltpu.CompilerParams(vmem_limit_bytes=50 * 1024 * 1024),
        name="channelize",
    )(x, taps, twiddle, second, keep)


def correlate_kernel(rows_ref, all_ref, out_ref):
    columns = rows_ref.shape[1] // 2
    for pair in range(2):
        at = slice(pair * columns, (pair + 1) * columns)
        out_ref[0, pair] = lax.dot_general(
            rows_ref[:, at], all_ref[:, at], (((1,), (1,)), ((), ())), preferred_element_type=F32
        ).astype(BF16)


def correlate(data, n_stn):
    signals, width = data.shape
    rows = signals // n_stn
    return pl.pallas_call(
        correlate_kernel,
        out_shape=jax.ShapeDtypeStruct((n_stn, 2, rows, signals), BF16),
        grid=(n_stn,),
        in_specs=[
            pl.BlockSpec((rows, width), lambda d: (d, 0)),
            pl.BlockSpec((signals, width), lambda d: (0, 0)),
        ],
        out_specs=pl.BlockSpec((1, 2, rows, signals), lambda d: (d, 0, 0, 0)),
        compiler_params=pltpu.CompilerParams(vmem_limit_bytes=50 * 1024 * 1024),
        name="correlate",
    )(data, data)


def body(voltages, filter_taps, station_flags):
    sig_dev, spec_dev, channels = voltages.shape
    n_freq, n_stn = lax.axis_size("freq"), lax.axis_size("stn")
    own = sig_dev // n_freq
    frames = n_freq * spec_dev
    flags = jnp.repeat(station_flags, 2, axis=0).astype(F32)
    at_freq, at_stn = lax.axis_index("freq"), lax.axis_index("stn")
    keep = lax.dynamic_slice_in_dim(flags, at_stn * sig_dev + at_freq * own, own, 0)
    keep = jnp.tile(keep, (1, LANES // frames))
    twiddle, second = transform_tables(channels, n_freq, n_stn)

    x = lax.all_to_all(voltages.reshape(n_freq, own, spec_dev, channels), "freq", split_axis=0, concat_axis=0, tiled=True)
    x = x.transpose(0, 2, 1, 3).reshape(frames, own, channels)
    kept = channelize(x, filter_taps, twiddle, second, keep)
    data = lax.all_to_all(kept, ("stn", "freq"), split_axis=0, concat_axis=0, tiled=True)
    sums = correlate(data, n_stn)
    sums = lax.all_to_all(sums, "stn", split_axis=0, concat_axis=0, tiled=True)
    own_flags = lax.dynamic_slice_in_dim(flags, at_stn * sig_dev, sig_dev, 0)
    counts = jnp.dot(own_flags, flags.T, precision=lax.Precision.HIGHEST)
    scale = 1.0 / (AVG * jnp.maximum(counts, 1.0))
    return sums.reshape(n_stn * 2, sig_dev, -1).astype(F32) * scale[None]


def solution(mesh):
    in_specs = (P("stn", "freq", None), P(), P())
    out_specs = P("freq", "stn", None)
    return jax.shard_map(body, mesh=mesh, in_specs=in_specs, out_specs=out_specs, check_vma=False)
```

```python
import math

import jax
import jax.numpy as jnp
import numpy as np
from jax import lax
from jax.experimental import pallas as pl
from jax.experimental.pallas import tpu as pltpu
from jax.sharding import PartitionSpec as P

AVG = 16
LANES = 128
BLOCK = 256
INNER = 256
F32 = jnp.float32
BF16 = jnp.bfloat16


def transform_tables(channels, n_freq, n_stn):
    j0 = np.arange(INNER, dtype=np.float64)
    k1 = np.arange(AVG, dtype=np.float64)
    phase = 2 * np.pi * k1[:, None] * j0[None, :] / channels + np.pi * j0[None, :] / (2 * channels)
    phase = phase + np.pi * (2 * k1[:, None] + 1) / (4 * channels)
    twiddle = np.stack([np.cos(phase), -np.sin(phase)]).astype(np.float32)
    groups = channels // AVG
    per_device = groups // (n_freq * n_stn)
    k2 = np.arange(groups).reshape(n_freq, n_stn, per_device).transpose(1, 0, 2).reshape(-1)
    phase = 2 * np.pi * (k2[:, None] * np.arange(INNER)[None, :] % INNER) / INNER
    phase = phase + 2 * np.pi * AVG * k2[:, None] / (4 * channels)
    scale = math.sqrt(2.0 / channels)
    exact = np.concatenate([np.cos(phase), np.sin(phase)], axis=1) * scale
    exact = jnp.asarray(exact.astype(np.float32))
    high = exact.astype(BF16)
    low = (exact - high.astype(F32)).astype(BF16)
    return jnp.asarray(twiddle), jnp.concatenate([high, high, low], axis=1)


def times(value, angle):
    c, s = math.cos(angle), math.sin(angle)
    re, im = value
    return re * c + im * s, im * c - re * s


def four_point(u0, u1, u2, u3):
    def add(a, b):
        return a[0] + b[0], a[1] + b[1]

    def sub(a, b):
        return a[0] - b[0], a[1] - b[1]

    s0, s1, t0, t1 = add(u0, u2), sub(u0, u2), add(u1, u3), sub(u1, u3)
    return add(s0, t0), (s1[0] + t1[1], s1[1] - t1[0]), sub(s0, t0), (s1[0] - t1[1], s1[1] + t1[0])


def sixteen_point(x):
    mid = []
    for b in range(4):
        u = [(x[b], jnp.zeros_like(x[b]))]
        for a in range(1, 4):
            angle = math.pi * a / 8
            u.append((x[4 * a + b] * math.cos(angle), x[4 * a + b] * -math.sin(angle)))
        row = four_point(*u)
        mid.append([times(row[p], 2 * math.pi * b * p / 16 + math.pi * b / 32) if b else row[p] for p in range(4)])
    y = [None] * 16
    for p in range(4):
        out = four_point(*[mid[b][p] for b in range(4)])
        for q in range(4):
            y[p + 4 * q] = out[q]
    return y


def channelize_kernel(x_ref, taps_ref, twiddle_ref, second_ref, keep_ref, out_ref, window, stage, turned):
    sources, signals, per_source, channels = x_ref.shape
    taps = taps_ref.shape[0]
    groups = second_ref.shape[0]
    rows = signals * per_source
    halves = INNER // LANES

    odd = lax.broadcasted_iota(jnp.int32, (rows, LANES), 0) % 2 == 1

    def fir(block, carry):
        lanes = pl.ds(pl.multiple_of(block * LANES, LANES), LANES)
        tap = [jnp.broadcast_to(taps_ref[pl.ds(t, 1), lanes], (rows, LANES)) for t in range(taps)]
        x = [x_ref[f, :, :, lanes].reshape(rows, LANES).astype(F32) for f in range(sources)]
        up = [pltpu.roll(v, rows - 1, 0) for v in x]
        down = [pltpu.roll(v, 1, 0) for v in x]
        late = [jnp.where(odd, down[f], up[f - 1] if f else 0.0) for f in range(sources)]
        for f in range(sources):
            total = tap[0] * x[f] + tap[1] * late[f]
            for u in range(1, min(taps // 2, f + 1)):
                total = total + tap[2 * u] * x[f - u] + tap[2 * u + 1] * late[f - u]
            window[f, :, lanes] = total
        return carry

    lax.fori_loop(0, channels // LANES, fir, 0)

    def first(f, carry):
        for half in range(halves):
            at = pl.ds(half * LANES, LANES)
            x = [window[f, :, pl.ds(j1 * INNER + half * LANES, LANES)] for j1 in range(AVG)]
            for k1, y in enumerate(sixteen_point(x)):
                tre = twiddle_ref[0, pl.ds(k1, 1), at]
                tim = twiddle_ref[1, pl.ds(k1, 1), at]
                to = pl.ds(pl.multiple_of((k1 * sources + f) * rows, rows), rows)
                stage[half, to, :] = y[0] * tre - y[1] * tim
                stage[halves + half, to, :] = y[0] * tim + y[1] * tre
        return carry

    lax.fori_loop(0, sources, first, 0)

    depth = AVG * sources
    columns = per_source * depth
    for s in range(signals):
        parts = [
            jnp.concatenate(
                [stage[part, pl.ds(s * per_source + i, depth, stride=rows), :] for part in range(2 * halves)], axis=1
            )
            for i in range(per_source)
        ]
        y = jnp.concatenate(parts, axis=0)
        high = y.astype(BF16)
        low = (y - high.astype(F32)).astype(BF16)
        z = lax.dot_general(
            second_ref[...],
            jnp.concatenate([high, low, high], axis=1),
            (((1,), (1,)), ((), ())),
            preferred_element_type=F32,
        )
        for c in range(columns // LANES):
            turned[c, pl.ds(s, groups, stride=signals), :] = z[:, c * LANES : (c + 1) * LANES]

    blocks = columns // LANES

    def last(step, carry):
        rows_in = pl.ds(pl.multiple_of(step * 32 * signals, 32 * signals), 32 * signals)
        to = pl.ds(pl.multiple_of(step * 16 * signals, 16 * signals), 16 * signals)
        for c in range(blocks):
            keep = keep_ref[c * per_source // blocks]
            value = turned[c, rows_in, :].reshape(16, 2, signals, LANES) * keep[None, None]
            for pair in range(2):
                part = value[:, pair].reshape(16 * signals, LANES).astype(BF16)
                out_ref[to, pair * columns + c * LANES : pair * columns + (c + 1) * LANES] = part
        return carry

    lax.fori_loop(0, groups // 32, last, 0)


def channelize(x, taps, twiddle, second, keep):
    sources, signals, per_source, channels = x.shape
    groups = channels // AVG
    columns = AVG * sources * per_source
    whole = pl.BlockSpec(memory_space=pltpu.VMEM)
    return pl.pallas_call(
        channelize_kernel,
        out_shape=jax.ShapeDtypeStruct((groups // 2 * signals, 2 * columns), BF16),
        in_specs=[whole] * 5,
        out_specs=whole,
        scratch_shapes=[
            pltpu.VMEM((sources, signals * per_source, channels), F32),
            pltpu.VMEM((4, AVG * sources * signals * per_source, LANES), F32),
            pltpu.VMEM((columns // LANES, groups * signals, LANES), F32),
        ],
        compiler_params=pltpu.CompilerParams(vmem_limit_bytes=28 * 1024 * 1024),
        name="channelize",
    )(x, taps, twiddle, second, keep)


def correlate_kernel(data_ref, out_ref):
    signals, width = data_ref.shape
    n_stn, pairs, rows, _ = out_ref.shape
    columns = width // pairs
    for pair in range(pairs):
        at = slice(pair * columns, (pair + 1) * columns)

        def block(c, carry):
            others = pl.ds(pl.multiple_of(c * BLOCK, BLOCK), BLOCK)
            sums = lax.dot_general(
                data_ref[:, at], data_ref[others, at], (((1,), (1,)), ((), ())), preferred_element_type=F32
            ).astype(BF16)
            out_ref[:, pair, :, others] = sums.reshape(n_stn, rows, BLOCK)
            return carry

        lax.fori_loop(0, signals // BLOCK, block, 0)


def correlate(data, n_stn):
    signals, width = data.shape
    whole = pl.BlockSpec(memory_space=pltpu.VMEM)
    return pl.pallas_call(
        correlate_kernel,
        out_shape=jax.ShapeDtypeStruct((n_stn, 2, signals // n_stn, signals), BF16),
        in_specs=[whole],
        out_specs=whole,
        compiler_params=pltpu.CompilerParams(vmem_limit_bytes=16 * 1024 * 1024),
        name="correlate",
    )(data)


def scale_kernel(sums_ref, scale_ref, out_ref):
    out_ref[...] = sums_ref[pl.program_id(0)].astype(F32)[None] * scale_ref[...]


def scaled(sums, scale):
    n, rows, signals = sums.shape
    whole = pl.BlockSpec(memory_space=pltpu.VMEM)
    return pl.pallas_call(
        scale_kernel,
        out_shape=jax.ShapeDtypeStruct((n, rows, signals), F32),
        grid=(n,),
        in_specs=[whole, whole],
        out_specs=pl.BlockSpec((1, rows, signals), lambda d: (d, 0, 0)),
        compiler_params=pltpu.CompilerParams(vmem_limit_bytes=16 * 1024 * 1024),
        name="scaled",
    )(sums, scale)


def body(voltages, filter_taps, station_flags):
    sig_dev, spec_dev, channels = voltages.shape
    n_freq, n_stn = lax.axis_size("freq"), lax.axis_size("stn")
    own = sig_dev // n_freq
    flags = jnp.repeat(station_flags, 2, axis=0).astype(F32)
    at_freq, at_stn = lax.axis_index("freq"), lax.axis_index("stn")
    keep = lax.dynamic_slice_in_dim(flags, at_stn * sig_dev + at_freq * own, own, 0)
    keep = keep.reshape(own, n_freq, spec_dev).transpose(2, 0, 1)
    keep = jnp.tile(keep, (1, 1, LANES // n_freq))
    twiddle, second = transform_tables(channels, n_freq, n_stn)

    x = lax.all_to_all(voltages.reshape(n_freq, own, spec_dev, channels), "freq", split_axis=0, concat_axis=0, tiled=True)
    kept = channelize(x, filter_taps, twiddle, second, keep)
    data = lax.all_to_all(kept, ("stn", "freq"), split_axis=0, concat_axis=0, tiled=True)
    sums = correlate(data, n_stn)
    sums = lax.all_to_all(sums, "stn", split_axis=0, concat_axis=0, tiled=True)
    own_flags = lax.dynamic_slice_in_dim(flags, at_stn * sig_dev, sig_dev, 0)
    counts = jnp.dot(own_flags, flags.T, precision=lax.Precision.HIGHEST)
    scale = 1.0 / (AVG * jnp.maximum(counts, 1.0))
    return scaled(sums.reshape(n_stn * 2, sig_dev, -1), scale)


def solution(mesh):
    in_specs = (P("stn", "freq", None), P(), P())
    out_specs = P("freq", "stn", None)
    return jax.shard_map(body, mesh=mesh, in_specs=in_specs, out_specs=out_specs, check_vma=False)
```

```python
import functools
import math

import jax
import jax.numpy as jnp
import numpy as np
from jax import lax
from jax.experimental import pallas as pl
from jax.experimental.pallas import tpu as pltpu
from jax.sharding import PartitionSpec as P

AVG = 16
LANES = 128
BLOCK = 256
TOGETHER = ((6,), (4,), (2,), (1,), (3,), (5,), (7,), (0,))
ARRIVING = ((0, 6), (4,), (2,), (1, 3, 5, 7))
INNER = 256
F32 = jnp.float32
BF16 = jnp.bfloat16


def transform_tables(channels, n_freq, n_stn):
    j0 = np.arange(INNER, dtype=np.float64)
    k1 = np.arange(AVG, dtype=np.float64)
    phase = 2 * np.pi * k1[:, None] * j0[None, :] / channels + np.pi * j0[None, :] / (2 * channels)
    phase = phase + np.pi * (2 * k1[:, None] + 1) / (4 * channels)
    twiddle = np.stack([np.cos(phase), -np.sin(phase)]).astype(np.float32)
    groups = channels // AVG
    per_device = groups // (n_freq * n_stn)
    k2 = np.arange(groups).reshape(n_freq, n_stn, per_device).transpose(1, 0, 2).reshape(-1)
    phase = 2 * np.pi * (k2[:, None] * np.arange(INNER)[None, :] % INNER) / INNER
    phase = phase + 2 * np.pi * AVG * k2[:, None] / (4 * channels)
    scale = math.sqrt(2.0 / channels)
    exact = np.concatenate([np.cos(phase), np.sin(phase)], axis=1) * scale
    exact = jnp.asarray(exact.astype(np.float32))
    high = exact.astype(BF16)
    low = (exact - high.astype(F32)).astype(BF16)
    twiddle, high, low = lax.optimization_barrier((jnp.asarray(twiddle), high, low))
    return jnp.stack([twiddle[0], twiddle[1]]), jnp.concatenate([high, high, low], axis=1)


def times(value, angle):
    c, s = math.cos(angle), math.sin(angle)
    re, im = value
    return re * c + im * s, im * c - re * s


def four_point(u0, u1, u2, u3):
    def add(a, b):
        return a[0] + b[0], a[1] + b[1]

    def sub(a, b):
        return a[0] - b[0], a[1] - b[1]

    s0, s1, t0, t1 = add(u0, u2), sub(u0, u2), add(u1, u3), sub(u1, u3)
    return add(s0, t0), (s1[0] + t1[1], s1[1] - t1[0]), sub(s0, t0), (s1[0] - t1[1], s1[1] + t1[0])


def sixteen_point(x):
    mid = []
    for b in range(4):
        u = [(x[b], jnp.zeros_like(x[b]))]
        for a in range(1, 4):
            angle = math.pi * a / 8
            u.append((x[4 * a + b] * math.cos(angle), x[4 * a + b] * -math.sin(angle)))
        row = four_point(*u)
        mid.append([times(row[p], 2 * math.pi * b * p / 16 + math.pi * b / 32) if b else row[p] for p in range(4)])
    y = [None] * 16
    for p in range(4):
        out = four_point(*[mid[b][p] for b in range(4)])
        for q in range(4):
            y[p + 4 * q] = out[q]
    return y


def channelize_kernel(
    x_ref, taps_hbm, keep_hbm, twiddle_hbm, second_hbm, out_hbm,
    window, stage_even, stage_odd, turned, out, taps_ref, keep_ref, twiddle_ref, second_ref, table_sems, out_sems,
):
    sources, signals, per_source, channels = x_ref.shape
    taps = taps_ref.shape[0]
    groups = second_ref.shape[0]
    frames = sources * per_source
    halves = INNER // LANES
    lane_blocks = channels // LANES
    chunk = 8 * LANES

    tables = [
        pltpu.make_async_copy(source, target, table_sems.at[n])
        for n, (source, target) in enumerate(
            ((taps_hbm, taps_ref), (keep_hbm, keep_ref), (twiddle_hbm, twiddle_ref), (second_hbm, second_ref))
        )
    ]
    for copy in tables:
        copy.start()
    tables[0].wait()

    def fir(step, carry):
        s = step // (channels // chunk)
        c = step % (channels // chunk)
        tap = [taps_ref[t, pl.ds(pl.multiple_of(c * 8, 8), 8), :] for t in range(taps)]
        x = []
        for f in range(sources):
            both = x_ref[f, s, :, pl.ds(pl.multiple_of(c * chunk, chunk), chunk)].astype(F32)
            for i in range(per_source):
                x.append(both[i : i + 1].reshape(8, LANES))
                m = f * per_source + i
                total, other = tap[0] * x[m], jnp.zeros((8, LANES), F32)
                for t in range(1, min(taps, m + 1)):
                    if t % 2:
                        other = other + tap[t] * x[m - t]
                    else:
                        total = total + tap[t] * x[m - t]
                window[pl.ds((s * frames + m) * (lane_blocks + 1) + c * 8, 8), :] = total + other
        return carry

    lax.fori_loop(0, signals * (channels // chunk), fir, 0)
    for copy in tables[1:]:
        copy.wait()

    columns = AVG * frames
    stages = (stage_even, stage_odd)

    def first(s):
        stage = stages[s % 2]
        for start in range(0, frames, 16):
            for half in range(halves):
                at = pl.ds(half * LANES, LANES)
                base = (s * frames + start) * (lane_blocks + 1) + half
                x = [window[pl.ds(base + j1 * halves, 16, stride=lane_blocks + 1), :] for j1 in range(AVG)]
                for k1, y in enumerate(sixteen_point(x)):
                    tre = twiddle_ref[0, pl.ds(k1, 1), at]
                    tim = twiddle_ref[1, pl.ds(k1, 1), at]
                    parts = (y[0] * tre - y[1] * tim, y[0] * tim + y[1] * tre)
                    for p, value in enumerate(parts):
                        high = value.astype(BF16)
                        low = (value - high.astype(F32)).astype(BF16)
                        to = pl.ds(k1 * frames + start, 16)
                        stage[to, pl.ds((p * halves + half) * LANES, LANES)] = high
                        stage[to, pl.ds((2 * halves + p * halves + half) * LANES, LANES)] = low

    def second(s):
        stage = stages[s % 2]
        width = 2 * INNER
        z = lax.dot_general(
            second_ref[...],
            jnp.concatenate([stage[...], stage[:, :width]], axis=1),
            (((1,), (1,)), ((), ())),
            preferred_element_type=F32,
        )
        for c in range(columns // LANES):
            turned[c, pl.ds(s, groups, stride=signals + 1), :] = z[:, c * LANES : (c + 1) * LANES]

    first(0)
    for s in range(signals):
        if s + 1 < signals:
            first(s + 1)
        second(s)

    keep = keep_ref[...]
    step_groups = 32
    step_rows = step_groups // 2 * signals

    def out_copy(step):
        rows = pl.ds(pl.multiple_of(step * step_rows, step_rows), step_rows)
        return pltpu.make_async_copy(out.at[rows, :], out_hbm.at[rows, :], out_sems.at[step])

    def last(step, carry):
        rows = pl.ds(pl.multiple_of(step * step_rows, step_rows), step_rows)
        for c in range(columns // LANES):
            for pair in range(2):
                value = jnp.concatenate(
                    [
                        turned[c, pl.ds((step * step_groups + g) * (signals + 1), signals), :] * keep
                        for g in range(pair, step_groups, 2)
                    ],
                    axis=0,
                )
                out[rows, pl.ds(pair * columns + c * LANES, LANES)] = value.astype(BF16)
        out_copy(step).start()
        return carry

    steps = groups // step_groups
    lax.fori_loop(0, steps, last, 0)
    for step in range(steps):
        out_copy(step).wait()


def channelize(x, taps, keep, twiddle, second):
    sources, signals, per_source, channels = x.shape
    groups = channels // AVG
    frames = sources * per_source
    columns = AVG * frames
    lane_blocks = channels // LANES
    whole = pl.BlockSpec(memory_space=pltpu.VMEM)
    hbm = pl.BlockSpec(memory_space=pltpu.HBM)
    shape = (groups // 2 * signals, 2 * columns)
    return pl.pallas_call(
        channelize_kernel,
        out_shape=jax.ShapeDtypeStruct(shape, BF16),
        in_specs=[whole] + [hbm] * 4,
        out_specs=hbm,
        scratch_shapes=[
            pltpu.VMEM((signals * frames * (lane_blocks + 1), LANES), F32),
            pltpu.VMEM((columns, 4 * INNER), BF16),
            pltpu.VMEM((columns, 4 * INNER), BF16),
            pltpu.VMEM((columns // LANES, groups * (signals + 1), LANES), F32),
            pltpu.VMEM(shape, BF16),
            pltpu.VMEM((taps.shape[0], lane_blocks, LANES), F32),
            pltpu.VMEM(keep.shape, F32),
            pltpu.VMEM(twiddle.shape, F32),
            pltpu.VMEM(second.shape, BF16),
            pltpu.SemaphoreType.DMA((4,)),
            pltpu.SemaphoreType.DMA((groups // 32,)),
        ],
        compiler_params=pltpu.CompilerParams(vmem_limit_bytes=28 * 1024 * 1024),
        name="channelize",
    )(x, taps.reshape(taps.shape[0], lane_blocks, LANES), keep, twiddle, second)


def correlate_kernel(to_ref, data_ref, *out_refs):
    pairs, rows, signals = out_refs[0].shape
    columns = data_ref.shape[1] // pairs
    for pair in range(pairs):
        at = slice(pair * columns, (pair + 1) * columns)
        own = [data_ref[pl.ds(pl.multiple_of(to_ref[n] * rows, rows), rows), at] for n in range(len(out_refs))]
        own = jnp.concatenate(own, axis=0)
        for c in range(signals // BLOCK):
            others = slice(c * BLOCK, (c + 1) * BLOCK)
            sums = lax.dot_general(own, data_ref[others, at], (((1,), (1,)), ((), ())), preferred_element_type=F32)
            for n, out_ref in enumerate(out_refs):
                out_ref[pair, :, others] = sums[n * rows : (n + 1) * rows].astype(BF16)


def correlate(data, to, n_stn):
    signals, width = data.shape
    rows = signals // n_stn
    whole = pl.BlockSpec(memory_space=pltpu.VMEM)
    return pl.pallas_call(
        correlate_kernel,
        out_shape=(jax.ShapeDtypeStruct((2, rows, signals), BF16),) * len(to),
        in_specs=[pl.BlockSpec(memory_space=pltpu.SMEM), whole],
        out_specs=(whole,) * len(to),
        compiler_params=pltpu.CompilerParams(vmem_limit_bytes=16 * 1024 * 1024),
        cost_estimate=pl.CostEstimate(
            flops=2 * len(to) * rows * signals * width, bytes_accessed=2 * signals * width, transcendentals=0
        ),
        name="correlate",
    )(jnp.stack(to).astype(jnp.int32), data)


def scale_kernel(at_ref, scale_ref, *refs):
    *tiles, out_ref = refs
    count = at_ref.shape[0]
    for n in range(count):

        @pl.when(pl.program_id(0) == n)
        def _():
            out_ref[...] = tiles[n][...].astype(F32) * scale_ref[...][None]


def scaled(tiles, scale, at, n_stn, buffer):
    pairs, rows, signals = tiles[0].shape
    extra = [] if buffer is None else [buffer]
    count = len(tiles)
    whole = pl.BlockSpec(memory_space=pltpu.VMEM)
    return pl.pallas_call(
        lambda at_ref, scale_ref, *refs: scale_kernel(at_ref, scale_ref, *refs[:count], refs[-1]),
        out_shape=jax.ShapeDtypeStruct((pairs * n_stn, rows, signals), F32),
        grid_spec=pltpu.PrefetchScalarGridSpec(
            num_scalar_prefetch=1,
            grid=(count, pairs),
            in_specs=[whole]
            + [pl.BlockSpec((1, rows, signals), functools.partial(tile_block, n, pairs)) for n in range(count)]
            + [pl.BlockSpec(memory_space=pl.ANY)] * len(extra),
            out_specs=pl.BlockSpec((1, rows, signals), lambda t, g, at: (pairs * at[t] + g, 0, 0)),
        ),
        input_output_aliases={2 + count: 0} if extra else {},
        compiler_params=pltpu.CompilerParams(vmem_limit_bytes=16 * 1024 * 1024),
        cost_estimate=pl.CostEstimate(
            flops=count * pairs * rows * signals, bytes_accessed=8 * count * pairs * rows * signals, transcendentals=0
        ),
        name="scaled",
    )(jnp.stack(at).astype(jnp.int32), scale, *tiles, *extra)


def tile_block(n, pairs, tile, pair, at_ref):
    return jnp.where(tile < n, 0, jnp.where(tile > n, pairs - 1, pair)), 0, 0


def body(voltages, filter_taps, station_flags):
    sig_dev, spec_dev, channels = voltages.shape
    n_freq, n_stn = lax.axis_size("freq"), lax.axis_size("stn")
    own = sig_dev // n_freq
    flags = jnp.repeat(station_flags, 2, axis=0).astype(F32)
    at_freq, at_stn = lax.axis_index("freq"), lax.axis_index("stn")
    keep = lax.dynamic_slice_in_dim(flags, at_stn * sig_dev + at_freq * own, own, 0)
    keep = jnp.tile(keep, (1, LANES // keep.shape[1]))
    twiddle, second = transform_tables(channels, n_freq, n_stn)

    x = lax.all_to_all(voltages.reshape(n_freq, own, spec_dev, channels), "freq", split_axis=0, concat_axis=0, tiled=True)
    kept = channelize(x, filter_taps, keep, twiddle, second)
    own_flags = lax.dynamic_slice_in_dim(flags, at_stn * sig_dev, sig_dev, 0)
    counts = jnp.dot(own_flags, flags.T, precision=lax.Precision.HIGHEST)
    scale = 1.0 / (AVG * jnp.maximum(counts, 1.0))
    partners = [at_stn ^ d for d in range(n_stn)]
    kept, scale, *partners = lax.optimization_barrier((kept, scale, *partners))
    data = lax.all_to_all(kept, ("stn", "freq"), split_axis=0, concat_axis=0, tiled=True)
    sent = {}
    for distances in TOGETHER:
        for distance, tile in zip(distances, correlate(data, [partners[d] for d in distances], n_stn)):
            route = [(i, i ^ distance) for i in range(n_stn)]
            sent[distance] = lax.ppermute(tile, "stn", route) if distance else tile
    result = None
    for distances in ARRIVING:
        result = scaled([sent[d] for d in distances], scale, [partners[d] for d in distances], n_stn, result)
    return result


def solution(mesh):
    in_specs = (P("stn", "freq", None), P(), P())
    out_specs = P("freq", "stn", None)
    return jax.shard_map(body, mesh=mesh, in_specs=in_specs, out_specs=out_specs, check_vma=False)
```

```python
import functools
import math

import jax
import jax.numpy as jnp
import numpy as np
from jax import lax
from jax.experimental import pallas as pl
from jax.experimental.pallas import tpu as pltpu
from jax.sharding import PartitionSpec as P

AVG = 16
LANES = 128
BLOCK = 256
TOGETHER = ((6,), (4,), (2,), (1,), (3,), (5,), (7,), (0,))
ARRIVING = ((0, 6), (4,), (2,), (1,), (3, 5, 7))
INNER = 256
F32 = jnp.float32
BF16 = jnp.bfloat16


def transform_tables(channels, n_freq, n_stn):
    j0 = np.arange(INNER, dtype=np.float64)
    k1 = np.arange(AVG, dtype=np.float64)
    phase = 2 * np.pi * k1[:, None] * j0[None, :] / channels + np.pi * j0[None, :] / (2 * channels)
    phase = phase + np.pi * (2 * k1[:, None] + 1) / (4 * channels)
    twiddle = np.stack([np.cos(phase), -np.sin(phase)]).astype(np.float32)
    groups = channels // AVG
    per_device = groups // (n_freq * n_stn)
    k2 = np.arange(groups).reshape(n_freq, n_stn, per_device).transpose(1, 0, 2).reshape(-1)
    phase = 2 * np.pi * (k2[:, None] * np.arange(INNER)[None, :] % INNER) / INNER
    phase = phase + 2 * np.pi * AVG * k2[:, None] / (4 * channels)
    scale = math.sqrt(2.0 / channels)
    exact = np.concatenate([np.cos(phase), np.sin(phase)], axis=1) * scale
    exact = jnp.asarray(exact.astype(np.float32))
    high = exact.astype(BF16)
    low = (exact - high.astype(F32)).astype(BF16)
    twiddle, high, low = lax.optimization_barrier((jnp.asarray(twiddle), high, low))
    return jnp.stack([twiddle[0], twiddle[1]]), jnp.concatenate([high, low], axis=0)


def times(value, angle):
    c, s = math.cos(angle), math.sin(angle)
    re, im = value
    return re * c + im * s, im * c - re * s


def four_point(u0, u1, u2, u3):
    def add(a, b):
        return a[0] + b[0], a[1] + b[1]

    def sub(a, b):
        return a[0] - b[0], a[1] - b[1]

    s0, s1, t0, t1 = add(u0, u2), sub(u0, u2), add(u1, u3), sub(u1, u3)
    return add(s0, t0), (s1[0] + t1[1], s1[1] - t1[0]), sub(s0, t0), (s1[0] - t1[1], s1[1] + t1[0])


def sixteen_point(x):
    mid = []
    for b in range(4):
        u = [(x[b], jnp.zeros_like(x[b]))]
        for a in range(1, 4):
            angle = math.pi * a / 8
            u.append((x[4 * a + b] * math.cos(angle), x[4 * a + b] * -math.sin(angle)))
        row = four_point(*u)
        mid.append([times(row[p], 2 * math.pi * b * p / 16 + math.pi * b / 32) if b else row[p] for p in range(4)])
    y = [None] * 16
    for p in range(4):
        out = four_point(*[mid[b][p] for b in range(4)])
        for q in range(4):
            y[p + 4 * q] = out[q]
    return y


def channelize_kernel(
    x_ref, rows_ref, keep_hbm, twiddle_hbm, second_hbm, out_hbm,
    window, stage_even, stage_odd, turned, out, taps_ref, keep_ref, twiddle_ref, second_ref, table_sems, out_sems,
):
    sources, signals, per_source, channels = x_ref.shape
    taps = taps_ref.shape[0]
    groups = second_ref.shape[0] // 2
    frames = sources * per_source
    halves = INNER // LANES
    lane_blocks = channels // LANES
    chunk = 8 * LANES

    tables = [
        pltpu.make_async_copy(source, target, table_sems.at[n])
        for n, (source, target) in enumerate(
            ((keep_hbm, keep_ref), (twiddle_hbm, twiddle_ref), (second_hbm, second_ref))
        )
    ]
    for copy in tables:
        copy.start()
    for t in range(taps):
        for c in range(channels // chunk):
            taps_ref[t, c * 8 : (c + 1) * 8, :] = rows_ref[t : t + 1, c * chunk : (c + 1) * chunk].reshape(8, LANES)

    def fir(step, carry):
        s = step // (channels // chunk)
        c = step % (channels // chunk)
        tap = [taps_ref[t, pl.ds(pl.multiple_of(c * 8, 8), 8), :] for t in range(taps)]
        x = []
        for f in range(sources):
            both = x_ref[f, s, :, pl.ds(pl.multiple_of(c * chunk, chunk), chunk)].astype(F32)
            for i in range(per_source):
                x.append(both[i : i + 1].reshape(8, LANES))
                m = f * per_source + i
                total, other = tap[0] * x[m], jnp.zeros((8, LANES), F32)
                for t in range(1, min(taps, m + 1)):
                    if t % 2:
                        other = other + tap[t] * x[m - t]
                    else:
                        total = total + tap[t] * x[m - t]
                window[pl.ds((s * frames + m) * (lane_blocks + 1) + c * 8, 8), :] = total + other
        return carry

    lax.fori_loop(0, signals * (channels // chunk), fir, 0)
    for copy in tables:
        copy.wait()

    columns = AVG * frames
    stages = (stage_even, stage_odd)

    def first(s):
        stage = stages[s % 2]
        for start in range(0, frames, 16):
            for half in range(halves):
                at = pl.ds(half * LANES, LANES)
                base = (s * frames + start) * (lane_blocks + 1) + half
                x = [window[pl.ds(base + j1 * halves, 16, stride=lane_blocks + 1), :] for j1 in range(AVG)]
                for k1, y in enumerate(sixteen_point(x)):
                    tre = twiddle_ref[0, pl.ds(k1, 1), at]
                    tim = twiddle_ref[1, pl.ds(k1, 1), at]
                    parts = (y[0] * tre - y[1] * tim, y[0] * tim + y[1] * tre)
                    for p, value in enumerate(parts):
                        high = value.astype(BF16)
                        low = (value - high.astype(F32)).astype(BF16)
                        to = pl.ds(k1 * frames + start, 16)
                        stage[to, pl.ds((p * halves + half) * LANES, LANES)] = high
                        stage[to, pl.ds((2 * halves + p * halves + half) * LANES, LANES)] = low

    def second(s):
        stage = stages[s % 2]
        width = 2 * INNER
        across = (((1,), (1,)), ((), ()))
        z = lax.dot_general(second_ref[...], stage[:, :width], across, preferred_element_type=F32)
        z = z[:groups] + z[groups:]
        z = z + lax.dot_general(second_ref[:groups], stage[:, width:], across, preferred_element_type=F32)
        for c in range(columns // LANES):
            turned[c, pl.ds(s, groups, stride=signals + 1), :] = z[:, c * LANES : (c + 1) * LANES]

    first(0)
    for s in range(signals):
        if s + 1 < signals:
            first(s + 1)
        second(s)

    keep = keep_ref[...]
    step_groups = 32
    step_rows = step_groups // 2 * signals

    def out_copy(step):
        rows = pl.ds(pl.multiple_of(step * step_rows, step_rows), step_rows)
        return pltpu.make_async_copy(out.at[rows, :], out_hbm.at[rows, :], out_sems.at[step])

    def last(step, carry):
        rows = pl.ds(pl.multiple_of(step * step_rows, step_rows), step_rows)
        for c in range(columns // LANES):
            for pair in range(2):
                value = jnp.concatenate(
                    [
                        turned[c, pl.ds((step * step_groups + g) * (signals + 1), signals), :] * keep
                        for g in range(pair, step_groups, 2)
                    ],
                    axis=0,
                )
                out[rows, pl.ds(pair * columns + c * LANES, LANES)] = value.astype(BF16)
        out_copy(step).start()
        return carry

    steps = groups // step_groups
    lax.fori_loop(0, steps, last, 0)
    for step in range(steps):
        out_copy(step).wait()


def channelize(x, taps, keep, twiddle, second):
    sources, signals, per_source, channels = x.shape
    groups = channels // AVG
    frames = sources * per_source
    columns = AVG * frames
    lane_blocks = channels // LANES
    whole = pl.BlockSpec(memory_space=pltpu.VMEM)
    hbm = pl.BlockSpec(memory_space=pltpu.HBM)
    shape = (groups // 2 * signals, 2 * columns)
    return pl.pallas_call(
        channelize_kernel,
        out_shape=jax.ShapeDtypeStruct(shape, BF16),
        in_specs=[whole] * 2 + [hbm] * 3,
        out_specs=hbm,
        scratch_shapes=[
            pltpu.VMEM((signals * frames * (lane_blocks + 1), LANES), F32),
            pltpu.VMEM((columns, 4 * INNER), BF16),
            pltpu.VMEM((columns, 4 * INNER), BF16),
            pltpu.VMEM((columns // LANES, groups * (signals + 1), LANES), F32),
            pltpu.VMEM(shape, BF16),
            pltpu.VMEM((taps.shape[0], lane_blocks, LANES), F32),
            pltpu.VMEM(keep.shape, F32),
            pltpu.VMEM(twiddle.shape, F32),
            pltpu.VMEM(second.shape, BF16),
            pltpu.SemaphoreType.DMA((3,)),
            pltpu.SemaphoreType.DMA((groups // 32,)),
        ],
        compiler_params=pltpu.CompilerParams(vmem_limit_bytes=28 * 1024 * 1024),
        name="channelize",
    )(x, taps, keep, twiddle, second)


def correlate_kernel(to_ref, data_ref, *out_refs):
    pairs, rows, signals = out_refs[0].shape
    columns = data_ref.shape[1] // pairs
    for pair in range(pairs):
        at = slice(pair * columns, (pair + 1) * columns)
        own = [data_ref[pl.ds(pl.multiple_of(to_ref[n] * rows, rows), rows), at] for n in range(len(out_refs))]
        own = jnp.concatenate(own, axis=0)
        for c in range(signals // BLOCK):
            others = slice(c * BLOCK, (c + 1) * BLOCK)
            sums = lax.dot_general(own, data_ref[others, at], (((1,), (1,)), ((), ())), preferred_element_type=F32)
            for n, out_ref in enumerate(out_refs):
                out_ref[pair, :, others] = sums[n * rows : (n + 1) * rows].astype(BF16)


def correlate(data, to, n_stn):
    signals, width = data.shape
    rows = signals // n_stn
    whole = pl.BlockSpec(memory_space=pltpu.VMEM)
    return pl.pallas_call(
        correlate_kernel,
        out_shape=(jax.ShapeDtypeStruct((2, rows, signals), BF16),) * len(to),
        in_specs=[pl.BlockSpec(memory_space=pltpu.SMEM), whole],
        out_specs=(whole,) * len(to),
        compiler_params=pltpu.CompilerParams(vmem_limit_bytes=16 * 1024 * 1024),
        cost_estimate=pl.CostEstimate(
            flops=2 * len(to) * rows * signals * width, bytes_accessed=2 * signals * width, transcendentals=0
        ),
        name="correlate",
    )(jnp.stack(to).astype(jnp.int32), data)


PARTS = 2


def scale_kernel(count, at_ref, scale_ref, *refs):
    tiles, (out_hbm, made, sems) = refs[:count], refs[-3:]
    _, pairs, rows, _ = made.shape
    part_rows = rows // PARTS
    copies = []
    for n in range(count):
        for pair in range(pairs):
            for part in range(PARTS):
                own = pl.ds(part * part_rows, part_rows)
                made[n, pair, own, :] = tiles[n][pair, own, :].astype(F32) * scale_ref[own, :]
                copy = pltpu.make_async_copy(
                    made.at[n, pair, own, :], out_hbm.at[pairs * at_ref[n] + pair, own, :], sems.at[len(copies)]
                )
                copy.start()
                copies.append(copy)
    for copy in copies:
        copy.wait()


def scaled(tiles, scale, at, n_stn, buffer):
    pairs, rows, signals = tiles[0].shape
    extra = [] if buffer is None else [buffer]
    count = len(tiles)
    whole = pl.BlockSpec(memory_space=pltpu.VMEM)
    return pl.pallas_call(
        functools.partial(scale_kernel, count),
        out_shape=jax.ShapeDtypeStruct((pairs * n_stn, rows, signals), F32),
        in_specs=[pl.BlockSpec(memory_space=pltpu.SMEM)]
        + [whole] * (1 + count)
        + [pl.BlockSpec(memory_space=pl.ANY)] * len(extra),
        out_specs=pl.BlockSpec(memory_space=pl.ANY),
        scratch_shapes=[
            pltpu.VMEM((count, pairs, rows, signals), F32),
            pltpu.SemaphoreType.DMA((count * pairs * PARTS,)),
        ],
        input_output_aliases={2 + count: 0} if extra else {},
        compiler_params=pltpu.CompilerParams(vmem_limit_bytes=16 * 1024 * 1024),
        cost_estimate=pl.CostEstimate(
            flops=count * pairs * rows * signals, bytes_accessed=8 * count * pairs * rows * signals, transcendentals=0
        ),
        name="scaled",
    )(jnp.stack(at).astype(jnp.int32), scale, *tiles, *extra)


def body(voltages, filter_taps, station_flags):
    sig_dev, spec_dev, channels = voltages.shape
    n_freq, n_stn = lax.axis_size("freq"), lax.axis_size("stn")
    own = sig_dev // n_freq
    flags = jnp.repeat(station_flags, 2, axis=0).astype(F32)
    at_freq, at_stn = lax.axis_index("freq"), lax.axis_index("stn")
    keep = lax.dynamic_slice_in_dim(flags, at_stn * sig_dev + at_freq * own, own, 0)
    keep = jnp.tile(keep, (1, LANES // keep.shape[1]))
    twiddle, second = transform_tables(channels, n_freq, n_stn)

    x = lax.all_to_all(voltages.reshape(n_freq, own, spec_dev, channels), "freq", split_axis=0, concat_axis=0, tiled=True)
    kept = channelize(x, filter_taps, keep, twiddle, second)
    own_flags = lax.dynamic_slice_in_dim(flags, at_stn * sig_dev, sig_dev, 0)
    counts = jnp.dot(own_flags, flags.T, precision=lax.Precision.HIGHEST)
    scale = 1.0 / (AVG * jnp.maximum(counts, 1.0))
    partners = [at_stn ^ d for d in range(n_stn)]
    kept, scale, *partners = lax.optimization_barrier((kept, scale, *partners))
    data = lax.all_to_all(kept, ("stn", "freq"), split_axis=0, concat_axis=0, tiled=True)
    sent = {}
    for distances in TOGETHER:
        for distance, tile in zip(distances, correlate(data, [partners[d] for d in distances], n_stn)):
            route = [(i, i ^ distance) for i in range(n_stn)]
            sent[distance] = lax.ppermute(tile, "stn", route) if distance else tile
    result = None
    for distances in ARRIVING:
        result = scaled([sent[d] for d in distances], scale, [partners[d] for d in distances], n_stn, result)
    return result


def solution(mesh):
    in_specs = (P("stn", "freq", None), P(), P())
    out_specs = P("freq", "stn", None)
    return jax.shard_map(body, mesh=mesh, in_specs=in_specs, out_specs=out_specs, check_vma=False)
```

```python
import functools
import math

import jax
import jax.numpy as jnp
import numpy as np
from jax import lax
from jax.experimental import pallas as pl
from jax.experimental.pallas import tpu as pltpu
from jax.sharding import PartitionSpec as P

AVG = 16
LANES = 128
BLOCK = 256
TOGETHER = ((6,), (4,), (2,), (1,), (3,), (7,), (5,), (0,))
ARRIVING = ((0, 6), (4,), (2,), (1,), (3, 7, 5))
INNER = 256
F32 = jnp.float32
BF16 = jnp.bfloat16


def transform_tables(channels, n_freq, n_stn):
    j0 = np.arange(INNER, dtype=np.float64)
    k1 = np.arange(AVG, dtype=np.float64)
    phase = 2 * np.pi * k1[:, None] * j0[None, :] / channels + np.pi * j0[None, :] / (2 * channels)
    phase = phase + np.pi * (2 * k1[:, None] + 1) / (4 * channels)
    twiddle = np.stack([np.cos(phase), -np.sin(phase)]).astype(np.float32)
    groups = channels // AVG
    per_device = groups // (n_freq * n_stn)
    k2 = np.arange(groups).reshape(n_freq, n_stn, per_device).transpose(1, 0, 2).reshape(-1)
    phase = 2 * np.pi * (k2[:, None] * np.arange(INNER)[None, :] % INNER) / INNER
    phase = phase + 2 * np.pi * AVG * k2[:, None] / (4 * channels)
    scale = math.sqrt(2.0 / channels)
    exact = np.concatenate([np.cos(phase), np.sin(phase)], axis=1) * scale
    exact = jnp.asarray(exact.astype(np.float32))
    high = exact.astype(BF16)
    low = (exact - high.astype(F32)).astype(BF16)
    twiddle, high, low = lax.optimization_barrier((jnp.asarray(twiddle), high, low))
    return jnp.stack([twiddle[0], twiddle[1]]), jnp.concatenate([high, low], axis=0)


def times(value, angle):
    c, s = math.cos(angle), math.sin(angle)
    re, im = value
    return re * c + im * s, im * c - re * s


def four_point(u0, u1, u2, u3):
    def add(a, b):
        return a[0] + b[0], a[1] + b[1]

    def sub(a, b):
        return a[0] - b[0], a[1] - b[1]

    s0, s1, t0, t1 = add(u0, u2), sub(u0, u2), add(u1, u3), sub(u1, u3)
    return add(s0, t0), (s1[0] + t1[1], s1[1] - t1[0]), sub(s0, t0), (s1[0] - t1[1], s1[1] + t1[0])


def sixteen_point(x):
    mid = []
    for b in range(4):
        u = [(x[b], jnp.zeros_like(x[b]))]
        for a in range(1, 4):
            angle = math.pi * a / 8
            u.append((x[4 * a + b] * math.cos(angle), x[4 * a + b] * -math.sin(angle)))
        row = four_point(*u)
        mid.append([times(row[p], 2 * math.pi * b * p / 16 + math.pi * b / 32) if b else row[p] for p in range(4)])
    y = [None] * 16
    for p in range(4):
        out = four_point(*[mid[b][p] for b in range(4)])
        for q in range(4):
            y[p + 4 * q] = out[q]
    return y


def channelize_kernel(
    x_ref, rows_ref, keep_hbm, twiddle_hbm, second_hbm, out,
    window, stage_even, stage_odd, turned, taps_ref, keep_ref, twiddle_ref, second_ref, table_sems,
):
    sources, signals, per_source, channels = x_ref.shape
    taps = taps_ref.shape[0]
    groups = second_ref.shape[0] // 2
    frames = sources * per_source
    halves = INNER // LANES
    lane_blocks = channels // LANES
    chunk = 8 * LANES

    tables = [
        pltpu.make_async_copy(source, target, table_sems.at[n])
        for n, (source, target) in enumerate(
            ((keep_hbm, keep_ref), (twiddle_hbm, twiddle_ref), (second_hbm, second_ref))
        )
    ]
    for copy in tables:
        copy.start()
    for t in range(taps):
        for c in range(channels // chunk):
            taps_ref[t, c * 8 : (c + 1) * 8, :] = rows_ref[t : t + 1, c * chunk : (c + 1) * chunk].reshape(8, LANES)

    def fir(step, carry):
        s = step // (channels // chunk)
        c = step % (channels // chunk)
        tap = [taps_ref[t, pl.ds(pl.multiple_of(c * 8, 8), 8), :] for t in range(taps)]
        x = []
        for f in range(sources):
            both = x_ref[f, s, :, pl.ds(pl.multiple_of(c * chunk, chunk), chunk)].astype(F32)
            for i in range(per_source):
                x.append(both[i : i + 1].reshape(8, LANES))
                m = f * per_source + i
                total, other = tap[0] * x[m], jnp.zeros((8, LANES), F32)
                for t in range(1, min(taps, m + 1)):
                    if t % 2:
                        other = other + tap[t] * x[m - t]
                    else:
                        total = total + tap[t] * x[m - t]
                window[pl.ds((s * frames + m) * (lane_blocks + 1) + c * 8, 8), :] = total + other
        return carry

    lax.fori_loop(0, signals * (channels // chunk), fir, 0)
    for copy in tables:
        copy.wait()

    columns = AVG * frames
    stages = (stage_even, stage_odd)

    def first(s):
        stage = stages[s % 2]
        for start in range(0, frames, 16):
            for half in range(halves):
                at = pl.ds(half * LANES, LANES)
                base = (s * frames + start) * (lane_blocks + 1) + half
                x = [window[pl.ds(base + j1 * halves, 16, stride=lane_blocks + 1), :] for j1 in range(AVG)]
                for k1, y in enumerate(sixteen_point(x)):
                    tre = twiddle_ref[0, pl.ds(k1, 1), at]
                    tim = twiddle_ref[1, pl.ds(k1, 1), at]
                    parts = (y[0] * tre - y[1] * tim, y[0] * tim + y[1] * tre)
                    for p, value in enumerate(parts):
                        high = value.astype(BF16)
                        low = (value - high.astype(F32)).astype(BF16)
                        to = pl.ds(k1 * frames + start, 16)
                        stage[to, pl.ds((p * halves + half) * LANES, LANES)] = high
                        stage[to, pl.ds((2 * halves + p * halves + half) * LANES, LANES)] = low

    def second(s):
        stage = stages[s % 2]
        width = 2 * INNER
        across = (((1,), (1,)), ((), ()))
        z = lax.dot_general(second_ref[...], stage[:, :width], across, preferred_element_type=F32)
        z = z[:groups] + z[groups:]
        z = z + lax.dot_general(second_ref[:groups], stage[:, width:], across, preferred_element_type=F32)
        for c in range(columns // LANES):
            turned[c, pl.ds(s, groups, stride=signals + 1), :] = z[:, c * LANES : (c + 1) * LANES]

    first(0)
    for s in range(signals):
        if s + 1 < signals:
            first(s + 1)
        second(s)

    keep = keep_ref[...]
    step_groups = 32
    step_rows = step_groups // 2 * signals

    def last(step, carry):
        rows = pl.ds(pl.multiple_of(step * step_rows, step_rows), step_rows)
        for c in range(columns // LANES):
            for pair in range(2):
                value = jnp.concatenate(
                    [
                        turned[c, pl.ds((step * step_groups + g) * (signals + 1), signals), :] * keep
                        for g in range(pair, step_groups, 2)
                    ],
                    axis=0,
                )
                out[rows, pl.ds(pair * columns + c * LANES, LANES)] = value.astype(BF16)
        return carry

    lax.fori_loop(0, groups // step_groups, last, 0)


def channelize(x, taps, keep, twiddle, second):
    sources, signals, per_source, channels = x.shape
    groups = channels // AVG
    frames = sources * per_source
    columns = AVG * frames
    lane_blocks = channels // LANES
    whole = pl.BlockSpec(memory_space=pltpu.VMEM)
    hbm = pl.BlockSpec(memory_space=pltpu.HBM)
    shape = (groups // 2 * signals, 2 * columns)
    return pl.pallas_call(
        channelize_kernel,
        out_shape=jax.ShapeDtypeStruct(shape, BF16),
        in_specs=[whole] * 2 + [hbm] * 3,
        out_specs=whole,
        scratch_shapes=[
            pltpu.VMEM((signals * frames * (lane_blocks + 1), LANES), F32),
            pltpu.VMEM((columns, 4 * INNER), BF16),
            pltpu.VMEM((columns, 4 * INNER), BF16),
            pltpu.VMEM((columns // LANES, groups * (signals + 1), LANES), F32),
            pltpu.VMEM((taps.shape[0], lane_blocks, LANES), F32),
            pltpu.VMEM(keep.shape, F32),
            pltpu.VMEM(twiddle.shape, F32),
            pltpu.VMEM(second.shape, BF16),
            pltpu.SemaphoreType.DMA((3,)),
        ],
        compiler_params=pltpu.CompilerParams(vmem_limit_bytes=28 * 1024 * 1024),
        name="channelize",
    )(x, taps, keep, twiddle, second)


def correlate_kernel(to_ref, data_ref, *out_refs):
    pairs, rows, signals = out_refs[0].shape
    columns = data_ref.shape[1] // pairs
    for pair in range(pairs):
        at = slice(pair * columns, (pair + 1) * columns)
        own = [data_ref[pl.ds(pl.multiple_of(to_ref[n] * rows, rows), rows), at] for n in range(len(out_refs))]
        own = jnp.concatenate(own, axis=0)
        for c in range(signals // BLOCK):
            others = slice(c * BLOCK, (c + 1) * BLOCK)
            sums = lax.dot_general(own, data_ref[others, at], (((1,), (1,)), ((), ())), preferred_element_type=F32)
            for n, out_ref in enumerate(out_refs):
                out_ref[pair, :, others] = sums[n * rows : (n + 1) * rows].astype(BF16)


def correlate(data, to, n_stn):
    signals, width = data.shape
    rows = signals // n_stn
    whole = pl.BlockSpec(memory_space=pltpu.VMEM)
    return pl.pallas_call(
        correlate_kernel,
        out_shape=(jax.ShapeDtypeStruct((2, rows, signals), BF16),) * len(to),
        in_specs=[pl.BlockSpec(memory_space=pltpu.SMEM), whole],
        out_specs=(whole,) * len(to),
        compiler_params=pltpu.CompilerParams(vmem_limit_bytes=16 * 1024 * 1024),
        cost_estimate=pl.CostEstimate(
            flops=2 * len(to) * rows * signals * width, bytes_accessed=2 * signals * width, transcendentals=0
        ),
        name="correlate",
    )(jnp.stack(to).astype(jnp.int32), data)


PARTS = 2


def scale_kernel(count, at_ref, scale_ref, *refs):
    tiles, (out_hbm, made, sems) = refs[:count], refs[-3:]
    _, pairs, rows, _ = made.shape
    part_rows = rows // PARTS
    copies = []
    for n in range(count):
        for pair in range(pairs):
            for part in range(PARTS):
                own = pl.ds(part * part_rows, part_rows)
                made[n, pair, own, :] = tiles[n][pair, own, :].astype(F32) * scale_ref[own, :]
                copy = pltpu.make_async_copy(
                    made.at[n, pair, own, :], out_hbm.at[pairs * at_ref[n] + pair, own, :], sems.at[len(copies)]
                )
                copy.start()
                copies.append(copy)
    for copy in copies:
        copy.wait()


def scaled(tiles, scale, at, n_stn, buffer):
    pairs, rows, signals = tiles[0].shape
    extra = [] if buffer is None else [buffer]
    count = len(tiles)
    whole = pl.BlockSpec(memory_space=pltpu.VMEM)
    return pl.pallas_call(
        functools.partial(scale_kernel, count),
        out_shape=jax.ShapeDtypeStruct((pairs * n_stn, rows, signals), F32),
        in_specs=[pl.BlockSpec(memory_space=pltpu.SMEM)]
        + [whole] * (1 + count)
        + [pl.BlockSpec(memory_space=pl.ANY)] * len(extra),
        out_specs=pl.BlockSpec(memory_space=pl.ANY),
        scratch_shapes=[
            pltpu.VMEM((count, pairs, rows, signals), F32),
            pltpu.SemaphoreType.DMA((count * pairs * PARTS,)),
        ],
        input_output_aliases={2 + count: 0} if extra else {},
        compiler_params=pltpu.CompilerParams(vmem_limit_bytes=16 * 1024 * 1024),
        cost_estimate=pl.CostEstimate(
            flops=count * pairs * rows * signals, bytes_accessed=8 * count * pairs * rows * signals, transcendentals=0
        ),
        name="scaled",
    )(jnp.stack(at).astype(jnp.int32), scale, *tiles, *extra)


def body(voltages, filter_taps, station_flags):
    sig_dev, spec_dev, channels = voltages.shape
    n_freq, n_stn = lax.axis_size("freq"), lax.axis_size("stn")
    own = sig_dev // n_freq
    flags = jnp.repeat(station_flags, 2, axis=0).astype(F32)
    at_freq, at_stn = lax.axis_index("freq"), lax.axis_index("stn")
    keep = lax.dynamic_slice_in_dim(flags, at_stn * sig_dev + at_freq * own, own, 0)
    keep = jnp.tile(keep, (1, LANES // keep.shape[1]))
    twiddle, second = transform_tables(channels, n_freq, n_stn)

    x = lax.all_to_all(voltages.reshape(n_freq, own, spec_dev, channels), "freq", split_axis=0, concat_axis=0, tiled=True)
    kept = channelize(x, filter_taps, keep, twiddle, second)
    own_flags = lax.dynamic_slice_in_dim(flags, at_stn * sig_dev, sig_dev, 0)
    counts = jnp.dot(own_flags, flags.T, precision=lax.Precision.HIGHEST)
    scale = 1.0 / (AVG * jnp.maximum(counts, 1.0))
    partners = [at_stn ^ d for d in range(n_stn)]
    kept, scale, *partners = lax.optimization_barrier((kept, scale, *partners))
    data = lax.all_to_all(kept, ("stn", "freq"), split_axis=0, concat_axis=0, tiled=True)
    sent = {}
    for distances in TOGETHER:
        for distance, tile in zip(distances, correlate(data, [partners[d] for d in distances], n_stn)):
            route = [(i, i ^ distance) for i in range(n_stn)]
            sent[distance] = lax.ppermute(tile, "stn", route) if distance else tile
    result = None
    for distances in ARRIVING:
        result = scaled([sent[d] for d in distances], scale, [partners[d] for d in distances], n_stn, result)
    return result


def solution(mesh):
    in_specs = (P("stn", "freq", None), P(), P())
    out_specs = P("freq", "stn", None)
    return jax.shard_map(body, mesh=mesh, in_specs=in_specs, out_specs=out_specs, check_vma=False)
```

```python
import functools
import math

import jax
import jax.numpy as jnp
import numpy as np
from jax import lax
from jax.experimental import pallas as pl
from jax.experimental.pallas import tpu as pltpu
from jax.sharding import PartitionSpec as P

AVG = 16
LANES = 128
BLOCK = 256
TOGETHER = ((6,), (4,), (2,), (1,), (3,), (7,), (5,), (0,))
ARRIVING = ((0, 6), (4,), (2,), (1,), (3, 7, 5))
INNER = 256
F32 = jnp.float32
BF16 = jnp.bfloat16


def transform_tables(channels, n_freq, n_stn):
    j0 = np.arange(INNER, dtype=np.float64)
    k1 = np.arange(AVG, dtype=np.float64)
    phase = 2 * np.pi * k1[:, None] * j0[None, :] / channels + np.pi * j0[None, :] / (2 * channels)
    phase = phase + np.pi * (2 * k1[:, None] + 1) / (4 * channels)
    twiddle = np.stack([np.cos(phase), -np.sin(phase)]).astype(np.float32)
    groups = channels // AVG
    per_device = groups // (n_freq * n_stn)
    k2 = np.arange(groups).reshape(n_freq, n_stn, per_device).transpose(1, 0, 2).reshape(-1)
    phase = 2 * np.pi * (k2[:, None] * np.arange(INNER)[None, :] % INNER) / INNER
    phase = phase + 2 * np.pi * AVG * k2[:, None] / (4 * channels)
    scale = math.sqrt(2.0 / channels)
    exact = np.concatenate([np.cos(phase), np.sin(phase)], axis=1) * scale
    exact = jnp.asarray(exact.astype(np.float32))
    high = exact.astype(BF16)
    low = (exact - high.astype(F32)).astype(BF16)
    twiddle, high, low = lax.optimization_barrier((jnp.asarray(twiddle), high, low))
    return jnp.stack([twiddle[0], twiddle[1]]), jnp.concatenate([high, low], axis=0)


def times(value, angle):
    c, s = math.cos(angle), math.sin(angle)
    re, im = value
    return re * c + im * s, im * c - re * s


def four_point(u0, u1, u2, u3):
    def add(a, b):
        return a[0] + b[0], a[1] + b[1]

    def sub(a, b):
        return a[0] - b[0], a[1] - b[1]

    s0, s1, t0, t1 = add(u0, u2), sub(u0, u2), add(u1, u3), sub(u1, u3)
    return add(s0, t0), (s1[0] + t1[1], s1[1] - t1[0]), sub(s0, t0), (s1[0] - t1[1], s1[1] + t1[0])


def sixteen_point(x):
    mid = []
    for b in range(4):
        u = [(x[b], jnp.zeros_like(x[b]))]
        for a in range(1, 4):
            angle = math.pi * a / 8
            u.append((x[4 * a + b] * math.cos(angle), x[4 * a + b] * -math.sin(angle)))
        row = four_point(*u)
        mid.append([times(row[p], 2 * math.pi * b * p / 16 + math.pi * b / 32) if b else row[p] for p in range(4)])
    y = [None] * 16
    for p in range(4):
        out = four_point(*[mid[b][p] for b in range(4)])
        for q in range(4):
            y[p + 4 * q] = out[q]
    return y


def channelize_kernel(
    x_ref, rows_ref, keep_ref, twiddle_ref, second_ref, out,
    window, stage_even, stage_odd, turned, taps_ref,
):
    sources, signals, per_source, channels = x_ref.shape
    taps = taps_ref.shape[0]
    groups = second_ref.shape[0] // 2
    frames = sources * per_source
    halves = INNER // LANES
    lane_blocks = channels // LANES
    chunk = 8 * LANES

    for t in range(taps):
        for c in range(channels // chunk):
            taps_ref[t, c * 8 : (c + 1) * 8, :] = rows_ref[t : t + 1, c * chunk : (c + 1) * chunk].reshape(8, LANES)

    def fir(step, carry):
        s = step // (channels // chunk)
        c = step % (channels // chunk)
        tap = [taps_ref[t, pl.ds(pl.multiple_of(c * 8, 8), 8), :] for t in range(taps)]
        x = []
        for f in range(sources):
            both = x_ref[f, s, :, pl.ds(pl.multiple_of(c * chunk, chunk), chunk)].astype(F32)
            for i in range(per_source):
                x.append(both[i : i + 1].reshape(8, LANES))
                m = f * per_source + i
                total, other = tap[0] * x[m], jnp.zeros((8, LANES), F32)
                for t in range(1, min(taps, m + 1)):
                    if t % 2:
                        other = other + tap[t] * x[m - t]
                    else:
                        total = total + tap[t] * x[m - t]
                window[pl.ds((s * frames + m) * (lane_blocks + 1) + c * 8, 8), :] = total + other
        return carry

    lax.fori_loop(0, signals * (channels // chunk), fir, 0)

    columns = AVG * frames
    stages = (stage_even, stage_odd)

    def first(s):
        stage = stages[s % 2]
        for start in range(0, frames, 16):
            for half in range(halves):
                at = pl.ds(half * LANES, LANES)
                base = (s * frames + start) * (lane_blocks + 1) + half
                x = [window[pl.ds(base + j1 * halves, 16, stride=lane_blocks + 1), :] for j1 in range(AVG)]
                for k1, y in enumerate(sixteen_point(x)):
                    tre = twiddle_ref[0, pl.ds(k1, 1), at]
                    tim = twiddle_ref[1, pl.ds(k1, 1), at]
                    parts = (y[0] * tre - y[1] * tim, y[0] * tim + y[1] * tre)
                    for p, value in enumerate(parts):
                        high = value.astype(BF16)
                        low = (value - high.astype(F32)).astype(BF16)
                        to = pl.ds(k1 * frames + start, 16)
                        stage[to, pl.ds((p * halves + half) * LANES, LANES)] = high
                        stage[to, pl.ds((2 * halves + p * halves + half) * LANES, LANES)] = low

    def second(s):
        stage = stages[s % 2]
        width = 2 * INNER
        across = (((1,), (1,)), ((), ()))
        z = lax.dot_general(second_ref[...], stage[:, :width], across, preferred_element_type=F32)
        z = z[:groups] + z[groups:]
        z = z + lax.dot_general(second_ref[:groups], stage[:, width:], across, preferred_element_type=F32)
        for c in range(columns // LANES):
            turned[c, pl.ds(s, groups, stride=signals + 1), :] = z[:, c * LANES : (c + 1) * LANES]

    first(0)
    for s in range(signals):
        if s + 1 < signals:
            first(s + 1)
        second(s)

    keep = keep_ref[...]
    step_groups = 32
    step_rows = step_groups // 2 * signals

    def last(step, carry):
        rows = pl.ds(pl.multiple_of(step * step_rows, step_rows), step_rows)
        for c in range(columns // LANES):
            for pair in range(2):
                value = jnp.concatenate(
                    [
                        turned[c, pl.ds((step * step_groups + g) * (signals + 1), signals), :] * keep
                        for g in range(pair, step_groups, 2)
                    ],
                    axis=0,
                )
                out[rows, pl.ds(pair * columns + c * LANES, LANES)] = value.astype(BF16)
        return carry

    lax.fori_loop(0, groups // step_groups, last, 0)


def channelize(x, taps, keep, twiddle, second):
    sources, signals, per_source, channels = x.shape
    groups = channels // AVG
    frames = sources * per_source
    columns = AVG * frames
    lane_blocks = channels // LANES
    whole = pl.BlockSpec(memory_space=pltpu.VMEM)
    shape = (groups // 2 * signals, 2 * columns)
    return pl.pallas_call(
        channelize_kernel,
        out_shape=jax.ShapeDtypeStruct(shape, BF16),
        in_specs=[whole] * 5,
        out_specs=whole,
        scratch_shapes=[
            pltpu.VMEM((signals * frames * (lane_blocks + 1), LANES), F32),
            pltpu.VMEM((columns, 4 * INNER), BF16),
            pltpu.VMEM((columns, 4 * INNER), BF16),
            pltpu.VMEM((columns // LANES, groups * (signals + 1), LANES), F32),
            pltpu.VMEM((taps.shape[0], lane_blocks, LANES), F32),
        ],
        compiler_params=pltpu.CompilerParams(vmem_limit_bytes=28 * 1024 * 1024),
        name="channelize",
    )(x, taps, keep, twiddle, second)


def correlate_kernel(to_ref, data_ref, *out_refs):
    pairs, rows, signals = out_refs[0].shape
    columns = data_ref.shape[1] // pairs
    for pair in range(pairs):
        at = slice(pair * columns, (pair + 1) * columns)
        own = [data_ref[pl.ds(pl.multiple_of(to_ref[n] * rows, rows), rows), at] for n in range(len(out_refs))]
        own = jnp.concatenate(own, axis=0)
        for c in range(signals // BLOCK):
            others = slice(c * BLOCK, (c + 1) * BLOCK)
            sums = lax.dot_general(own, data_ref[others, at], (((1,), (1,)), ((), ())), preferred_element_type=F32)
            for n, out_ref in enumerate(out_refs):
                out_ref[pair, :, others] = sums[n * rows : (n + 1) * rows].astype(BF16)


def correlate(data, to, n_stn):
    signals, width = data.shape
    rows = signals // n_stn
    whole = pl.BlockSpec(memory_space=pltpu.VMEM)
    return pl.pallas_call(
        correlate_kernel,
        out_shape=(jax.ShapeDtypeStruct((2, rows, signals), BF16),) * len(to),
        in_specs=[pl.BlockSpec(memory_space=pltpu.SMEM), whole],
        out_specs=(whole,) * len(to),
        compiler_params=pltpu.CompilerParams(vmem_limit_bytes=16 * 1024 * 1024),
        cost_estimate=pl.CostEstimate(
            flops=2 * len(to) * rows * signals * width, bytes_accessed=2 * signals * width, transcendentals=0
        ),
        name="correlate",
    )(jnp.stack(to).astype(jnp.int32), data)


PARTS = 2


def scale_kernel(count, at_ref, scale_ref, *refs):
    tiles, (out_hbm, made, sems) = refs[:count], refs[-3:]
    _, pairs, rows, _ = made.shape
    part_rows = rows // PARTS
    copies = []
    for n in range(count):
        for pair in range(pairs):
            for part in range(PARTS):
                own = pl.ds(part * part_rows, part_rows)
                made[n, pair, own, :] = tiles[n][pair, own, :].astype(F32) * scale_ref[own, :]
                copy = pltpu.make_async_copy(
                    made.at[n, pair, own, :], out_hbm.at[pairs * at_ref[n] + pair, own, :], sems.at[len(copies)]
                )
                copy.start()
                copies.append(copy)
    for copy in copies:
        copy.wait()


def scaled(tiles, scale, at, n_stn, buffer):
    pairs, rows, signals = tiles[0].shape
    extra = [] if buffer is None else [buffer]
    count = len(tiles)
    whole = pl.BlockSpec(memory_space=pltpu.VMEM)
    return pl.pallas_call(
        functools.partial(scale_kernel, count),
        out_shape=jax.ShapeDtypeStruct((pairs * n_stn, rows, signals), F32),
        in_specs=[pl.BlockSpec(memory_space=pltpu.SMEM)]
        + [whole] * (1 + count)
        + [pl.BlockSpec(memory_space=pl.ANY)] * len(extra),
        out_specs=pl.BlockSpec(memory_space=pl.ANY),
        scratch_shapes=[
            pltpu.VMEM((count, pairs, rows, signals), F32),
            pltpu.SemaphoreType.DMA((count * pairs * PARTS,)),
        ],
        input_output_aliases={2 + count: 0} if extra else {},
        compiler_params=pltpu.CompilerParams(vmem_limit_bytes=16 * 1024 * 1024),
        cost_estimate=pl.CostEstimate(
            flops=count * pairs * rows * signals, bytes_accessed=8 * count * pairs * rows * signals, transcendentals=0
        ),
        name="scaled",
    )(jnp.stack(at).astype(jnp.int32), scale, *tiles, *extra)


def body(voltages, filter_taps, station_flags):
    sig_dev, spec_dev, channels = voltages.shape
    n_freq, n_stn = lax.axis_size("freq"), lax.axis_size("stn")
    own = sig_dev // n_freq
    flags = jnp.repeat(station_flags, 2, axis=0).astype(F32)
    at_freq, at_stn = lax.axis_index("freq"), lax.axis_index("stn")
    keep = lax.dynamic_slice_in_dim(flags, at_stn * sig_dev + at_freq * own, own, 0)
    keep = jnp.tile(keep, (1, LANES // keep.shape[1]))
    twiddle, second = transform_tables(channels, n_freq, n_stn)

    x = lax.all_to_all(voltages.reshape(n_freq, own, spec_dev, channels), "freq", split_axis=0, concat_axis=0, tiled=True)
    kept = channelize(x, filter_taps, keep, twiddle, second)
    own_flags = lax.dynamic_slice_in_dim(flags, at_stn * sig_dev, sig_dev, 0)
    counts = jnp.dot(own_flags, flags.T, precision=lax.Precision.HIGHEST)
    scale = 1.0 / (AVG * jnp.maximum(counts, 1.0))
    partners = [at_stn ^ d for d in range(n_stn)]
    kept, scale, *partners = lax.optimization_barrier((kept, scale, *partners))
    data = lax.all_to_all(kept, ("stn", "freq"), split_axis=0, concat_axis=0, tiled=True)
    sent = {}
    for distances in TOGETHER:
        for distance, tile in zip(distances, correlate(data, [partners[d] for d in distances], n_stn)):
            route = [(i, i ^ distance) for i in range(n_stn)]
            sent[distance] = lax.ppermute(tile, "stn", route) if distance else tile
    result = None
    for distances in ARRIVING:
        result = scaled([sent[d] for d in distances], scale, [partners[d] for d in distances], n_stn, result)
    return result


def solution(mesh):
    in_specs = (P("stn", "freq", None), P(), P())
    out_specs = P("freq", "stn", None)
    return jax.shard_map(body, mesh=mesh, in_specs=in_specs, out_specs=out_specs, check_vma=False)
```
